32 devices in a mesh: section: 2 (over x), fsdp: 8 (over z, y), dp: 2 (over core).
Axes of the slice: x: 2, y: 2, z: 4, core: 2. Of those that a mesh axis runs over, the one named last changes fastest.
Arguments:
- hidden: bfloat16 [4, 512, 8192], P(('section', 'dp'), 'fsdp'), may hold values from -7 to 7
- cotangent: bfloat16 [4, 512, 8192], P(('section', 'dp'), None, 'fsdp'), may hold values from -6 to 6
- seg_ids: int32 [4, 512], P(('section', 'dp')), may hold values from 0 to 8, as said below
- advantage: float32 [4, 8], P(('section', 'dp')), may hold values from -4 to 4
- w_query: bfloat16 [8192, 8192], P('fsdp'), may hold values from -6 to 6
- w_key: bfloat16 [8192, 1024], P('fsdp'), may hold values from -6 to 6
- w_value: bfloat16 [8192, 1024], P('fsdp'), may hold values from -6 to 6
Outputs:
- rollout_query: bfloat16 [8192, 8192], P(None, 'fsdp')
- rollout_key: bfloat16 [8192, 1024], P(None, 'fsdp')
- rollout_value: bfloat16 [8192, 1024], P(None, 'fsdp')
The draws below stay inside these ranges and needn't reach their ends.
Inputs may be any that keep to these rules, and one draw needn't show every extreme that they name: `seg_ids`: in each block ids never fall; each id below 8 covers 1 to 64 positions, one of them exactly 64, and every id below 8 appears; id 8 marks padding at the block's end.
All inputs are finite; a program needn't handle non-finite values.
Results may differ from the reference program's by a relative error of at most 0.015.
The reference program's roundings to bfloat16 on the way (of `normed`, `attention_bf`, `grad_context` and `dscore`) count: a program that leaves them out, or rounds other values in their place, can miss the bound.
Values may be sent and summed in bfloat16 or wider, within the bound.
A program may use at most 192 MiB of HBM per device.

```python
import jax
import jax.numpy as jnp
from jax import lax

D = 8192
H = 64
KVH = 8
HD = 128
BLOCK = 512
RESP = 8
SHARE = 1
QPK = 8
COPIES = 8
MOST = 64
GROUPS = 4


def draw_seg_ids(key, part):
    divisors = jax.random.randint(jax.random.fold_in(key, 11), (GROUPS, RESP), 1, 9)
    lengths = MOST // divisors
    chosen = jax.random.randint(jax.random.fold_in(key, 12), (GROUPS, 1), 0, RESP)
    lengths = jnp.where(jnp.arange(RESP)[None, :] == chosen, MOST, lengths)
    ends = jnp.cumsum(lengths, axis=1)
    places = jnp.arange(BLOCK)
    return jnp.sum((places[None, :, None] >= ends[:, None, :]).astype(jnp.int32), axis=2).astype(jnp.int32)


def draw_hidden(key, part):
    field = jax.random.truncated_normal(jax.random.fold_in(key, 21), -6.0, 6.0, (GROUPS, BLOCK, D), jnp.float32)
    return field.astype(jnp.bfloat16)


def draw_w_query(key, part):
    field = jax.random.truncated_normal(jax.random.fold_in(key, 31), -6.0, 6.0, (D, H * HD), jnp.float32)
    return field.astype(jnp.bfloat16)


def draw_w_key(key, part):
    field = jax.random.truncated_normal(jax.random.fold_in(key, 41), -6.0, 6.0, (D, KVH * HD), jnp.float32)
    return field.astype(jnp.bfloat16)


def block_levels(stream_key, shape, cuts, low, high):
    factor_of = 1.0
    for axis_at, shards_of in cuts:
        steps = jax.random.uniform(jax.random.fold_in(jax.random.fold_in(stream_key, 6), axis_at), (shards_of,), jnp.float32, low / len(cuts), high / len(cuts))
        factor_of = factor_of * jnp.repeat(jnp.exp(steps), shape[axis_at] // shards_of).reshape((-1,) + (1,) * (len(shape) - 1 - axis_at))
    return factor_of


def normal_values(key, extent, width, most, shards=(), kind=jnp.bfloat16):
    entries = width * jax.random.normal(key, extent, jnp.float32)
    if shards:
        entries = entries * block_levels(key, extent, shards, -0.22, 0.18)
    return jnp.clip(entries, -most, most).astype(kind)


def setup_inputs(seed: int = 0) -> dict:
    keys = jax.random.split(jax.random.key(seed), 8)
    return {
        "hidden": draw_hidden(jax.random.fold_in(keys[7], 71), 0),
        "cotangent": normal_values(keys[1], (GROUPS, BLOCK, H * HD), 1.0, 6.0, ((0, 4), (2, 8))),
        "seg_ids": draw_seg_ids(jax.random.fold_in(keys[7], 71), 0),
        "advantage": normal_values(keys[3], (GROUPS, RESP), 1.0, 4.0, ((0, 4),), jnp.float32),
        "w_query": draw_w_query(jax.random.fold_in(keys[7], 71), 0),
        "w_key": draw_w_key(jax.random.fold_in(keys[7], 71), 0),
        "w_value": normal_values(keys[6], (D, KVH * HD), 1.0, 6.0, ((0, 8),)),
    }


step_rate = 200.0
rope_base = 1000000.0
norm_eps = 1e-06
masked_score = -1e+30

def rotate(field, cosine_table, sine_table):
    half_width = field.shape[-1] // 2
    lead_half = field[..., :half_width]
    tail_half = field[..., half_width:]
    return jnp.concatenate([lead_half * cosine_table - tail_half * sine_table, tail_half * cosine_table + lead_half * sine_table], -1)

def unrotate(field, cosine_table, sine_table):
    half_width = field.shape[-1] // 2
    lead_half = field[..., :half_width]
    tail_half = field[..., half_width:]
    return jnp.concatenate([lead_half * cosine_table + tail_half * sine_table, tail_half * cosine_table - lead_half * sine_table], -1)

def angles(seg_row):
    span_count = seg_row.shape[0]
    earlier = lax.optimization_barrier(jnp.sum((seg_row[None, :] < seg_row[:, None]).astype(jnp.int32), axis=1))
    positions = jnp.arange(span_count, dtype=jnp.int32) - earlier
    frequency = rope_base ** (-jnp.arange(HD // 2, dtype=jnp.float32) * 2.0 / HD)
    phase_grid = positions.astype(jnp.float32)[:, None] * frequency[None, :]
    return (jnp.cos(phase_grid)[:, None, :], jnp.sin(phase_grid)[:, None, :])

def token_weights(seg_row, advantage_row):
    id_range = jnp.arange(RESP + 1, dtype=jnp.int32)
    onehot = (seg_row[:, None] == id_range[None, :]).astype(jnp.float32)
    counts = lax.optimization_barrier(jnp.sum(onehot, axis=0))[:RESP]
    per_token = -advantage_row.astype(jnp.float32) / counts
    return lax.optimization_barrier(jnp.sum(onehot[:, :RESP] * per_token[None, :], axis=1))

def attend_back(q_rot, k_rot, v_bf, grad_context, allowed):
    highest = lax.Precision.HIGHEST
    score_scale = HD ** (-0.5)
    query_f = q_rot.astype(jnp.float32)
    key_f = k_rot.astype(jnp.float32)
    value_f = v_bf.astype(jnp.float32)
    context_f = grad_context.astype(jnp.float32)
    scores = jnp.einsum('tkjqd,ukd->kjqtu', query_f, key_f, precision=highest) * score_scale
    scores = jnp.where(allowed, scores, masked_score)
    row_top = lax.optimization_barrier(jnp.max(scores, axis=-1, keepdims=True))
    exponent = jnp.exp(scores - row_top)
    attention = exponent / lax.optimization_barrier(jnp.sum(exponent, axis=-1, keepdims=True))
    attention_bf = attention.astype(jnp.bfloat16)
    grad_prob = jnp.einsum('tkjqd,ukd->kjqtu', context_f, value_f, precision=highest)
    inner_sum = lax.optimization_barrier(jnp.sum(attention * grad_prob, axis=-1, keepdims=True))
    dscore = (attention * (grad_prob - inner_sum)).astype(jnp.bfloat16).astype(jnp.float32)
    grad_query = jnp.einsum('kjqtu,ukd->tkjqd', dscore, key_f, precision=highest) * score_scale
    grad_key = jnp.einsum('kjqtu,tkjqd->ukjd', dscore, query_f, precision=highest) * score_scale
    grad_value = jnp.einsum('kjqtu,tkjqd->ukjd', attention_bf.astype(jnp.float32), context_f, precision=highest)
    return (grad_query, grad_key, grad_value)

def rounded(field):
    return lax.optimization_barrier(field.astype(jnp.bfloat16)).astype(jnp.float32)

def reference(hidden, cotangent, seg_ids, advantage, w_query, w_key, w_value):
    inv_width = D ** (-0.5)
    block_len = BLOCK
    total_q = jnp.zeros((D, H * HD), jnp.float32)
    total_k = jnp.zeros((D, KVH * HD), jnp.float32)
    total_v = jnp.zeros((D, KVH * HD), jnp.float32)
    for group_index in range(GROUPS):
        token_rows = hidden[group_index].astype(jnp.float32)
        normed = (token_rows * lax.rsqrt(lax.optimization_barrier(jnp.mean(token_rows * token_rows, axis=-1, keepdims=True)) + norm_eps)).astype(jnp.bfloat16)
        queries = jnp.dot(normed, w_query, preferred_element_type=jnp.float32) * inv_width
        key_proj = jnp.dot(normed, w_key, preferred_element_type=jnp.float32) * inv_width
        value_proj = jnp.dot(normed, w_value, preferred_element_type=jnp.float32) * inv_width
        seg_row = seg_ids[group_index]
        cosine_table, sine_table = angles(seg_row)
        q_rot = rotate(queries.reshape(block_len, H, HD), cosine_table, sine_table).astype(jnp.bfloat16)
        k_rot = rotate(key_proj.reshape(block_len, KVH, HD), cosine_table, sine_table).astype(jnp.bfloat16)
        v_bf = value_proj.astype(jnp.bfloat16).reshape(block_len, KVH, HD)
        weight_row = token_weights(seg_row, advantage[group_index])
        grad_context = (cotangent[group_index].astype(jnp.float32) * weight_row[:, None]).astype(jnp.bfloat16)
        place = jnp.arange(block_len, dtype=jnp.int32)
        allowed = (seg_row[:, None] == seg_row[None, :]) & (place[None, :] <= place[:, None])
        grad_query, grad_key, grad_value = attend_back(q_rot.reshape(block_len, KVH, SHARE, QPK, HD), k_rot, v_bf, grad_context.reshape(block_len, KVH, SHARE, QPK, HD), allowed)
        grad_query = unrotate(grad_query.reshape(block_len, H, HD), cosine_table, sine_table)
        grad_key = unrotate(grad_key.reshape(block_len, COPIES, HD), cosine_table, sine_table)
        scaled_q = (grad_query.reshape(block_len, H * HD) * inv_width).astype(jnp.bfloat16)
        scaled_k = (grad_key.reshape(block_len, COPIES * HD) * inv_width).astype(jnp.bfloat16)
        scaled_v = (grad_value.reshape(block_len, COPIES * HD) * inv_width).astype(jnp.bfloat16)
        part_q = rounded(jnp.dot(normed.T, scaled_q, preferred_element_type=jnp.float32))
        part_k = rounded(jnp.dot(normed.T, scaled_k, preferred_element_type=jnp.float32))
        part_v = rounded(jnp.dot(normed.T, scaled_v, preferred_element_type=jnp.float32))
        total_q = total_q + part_q
        total_k = total_k + lax.optimization_barrier(jnp.sum(part_k.reshape(D, KVH, SHARE, HD), axis=2)).reshape(D, KVH * HD)
        total_v = total_v + lax.optimization_barrier(jnp.sum(part_v.reshape(D, KVH, SHARE, HD), axis=2)).reshape(D, KVH * HD)
    new_q = (w_query.astype(jnp.float32) - step_rate * total_q).astype(jnp.bfloat16)
    new_k = (w_key.astype(jnp.float32) - step_rate * total_k).astype(jnp.bfloat16)
    new_v = (w_value.astype(jnp.float32) - step_rate * total_v).astype(jnp.bfloat16)
    rollout_key = jnp.repeat(new_k.reshape(D, KVH, HD), SHARE, axis=1).reshape(D, COPIES * HD)
    rollout_value = jnp.repeat(new_v.reshape(D, KVH, HD), SHARE, axis=1).reshape(D, COPIES * HD)
    return (new_q, rollout_key, rollout_value)
```

```python
import functools

import jax
import jax.numpy as jnp
from jax import lax
from jax.experimental import pallas as pl
from jax.experimental.pallas import tpu as pltpu
from jax.sharding import PartitionSpec as P

D = 8192
H = 64
KVH = 8
HD = 128
RESP = 8


step_rate = 200.0
rope_base = 1000000.0
norm_eps = 1e-06
masked_score = -1e30


def rotate(field, cosine_table, sine_table):
    half_width = field.shape[-1] // 2
    lead_half = field[..., :half_width]
    tail_half = field[..., half_width:]
    return jnp.concatenate(
        [
            lead_half * cosine_table - tail_half * sine_table,
            tail_half * cosine_table + lead_half * sine_table,
        ],
        -1,
    )


def unrotate(field, cosine_table, sine_table):
    half_width = field.shape[-1] // 2
    lead_half = field[..., :half_width]
    tail_half = field[..., half_width:]
    return jnp.concatenate(
        [
            lead_half * cosine_table + tail_half * sine_table,
            tail_half * cosine_table - lead_half * sine_table,
        ],
        -1,
    )


def angles(seg_row):
    span_count = seg_row.shape[0]
    earlier = jnp.sum((seg_row[None, :] < seg_row[:, None]).astype(jnp.int32), axis=1)
    positions = jnp.arange(span_count, dtype=jnp.int32) - earlier
    frequency = rope_base ** (-jnp.arange(HD // 2, dtype=jnp.float32) * 2.0 / HD)
    phase_grid = positions.astype(jnp.float32)[:, None] * frequency[None, :]
    return (jnp.cos(phase_grid)[:, None, :], jnp.sin(phase_grid)[:, None, :])


def token_weights(seg_row, advantage_row):
    id_range = jnp.arange(RESP + 1, dtype=jnp.int32)
    onehot = (seg_row[:, None] == id_range[None, :]).astype(jnp.float32)
    counts = jnp.sum(onehot, axis=0)[:RESP]
    per_token = -advantage_row / counts
    return jnp.sum(onehot[:, :RESP] * per_token[None, :], axis=1)


def attend_back(q_rot, k_rot, v_bf, grad_context, allowed):
    score_scale = HD ** (-0.5)
    scores = (
        jnp.einsum("tkjqd,ukd->kjqtu", q_rot, k_rot, preferred_element_type=jnp.float32)
        * score_scale
    )
    scores = jnp.where(allowed, scores, masked_score)
    row_top = jnp.max(scores, axis=-1, keepdims=True)
    exponent = jnp.exp(scores - row_top)
    attention = exponent / jnp.sum(exponent, axis=-1, keepdims=True)
    attention_bf = attention.astype(jnp.bfloat16)
    grad_prob = jnp.einsum(
        "tkjqd,ukd->kjqtu", grad_context, v_bf, preferred_element_type=jnp.float32
    )
    inner_sum = jnp.sum(attention * grad_prob, axis=-1, keepdims=True)
    dscore = (attention * (grad_prob - inner_sum)).astype(jnp.bfloat16)
    grad_query = (
        jnp.einsum("kjqtu,ukd->tkjqd", dscore, k_rot, preferred_element_type=jnp.float32)
        * score_scale
    )
    grad_key = (
        jnp.einsum("kjqtu,tkjqd->ukjd", dscore, q_rot, preferred_element_type=jnp.float32)
        * score_scale
    )
    grad_value = jnp.einsum(
        "kjqtu,tkjqd->ukjd", attention_bf, grad_context, preferred_element_type=jnp.float32
    )
    return (grad_query, grad_key, grad_value)

MESH = pl.DeviceIdType.MESH


def remote(src, dst, send, recv, device):
    return pltpu.make_async_remote_copy(
        src_ref=src, dst_ref=dst, send_sem=send, recv_sem=recv, device_id=device, device_id_type=MESH
    )


def gather_kernel(
    count, share, n_ref, wq_ref, wkv_ref, hid_ref, qc_ref, kv_ref,
    w_send, w_recv, z_send, z_recv, y_send, y_recv, x_send, x_recv, g_send, g_recv, c_send, c_recv,
    own_sem,
):
    s, f, d = lax.axis_index("section"), lax.axis_index("fsdp"), lax.axis_index("dp")
    line = count // 2
    a, b = f // 2, f % 2
    to_y, to_x, to_c = {"fsdp": a * 2 + 1 - b}, {"section": 1 - s}, {"dp": 1 - d}
    rows = wq_ref.shape[0]
    part = rows // 4
    mine, across = s * 2 + d, (1 - s) * 2 + d
    pairs = ((wq_ref, qc_ref), (wkv_ref, kv_ref))
    via_x = line // 4

    barrier = pltpu.get_barrier_semaphore()

    def greet(k, carry):
        pl.semaphore_signal(barrier, inc=1, device_id={"fsdp": (f + k) % count}, device_id_type=MESH)
        return carry

    lax.fori_loop(1, count, greet, 0)
    pl.semaphore_signal(barrier, inc=1, device_id=to_x, device_id_type=MESH)
    pl.semaphore_signal(barrier, inc=1, device_id=to_c, device_id_type=MESH)
    pl.semaphore_wait(barrier, count + 1)

    def columns(i, target):
        wide = pairs[i][1].shape[1]
        at = target if i == 0 else target // share
        return pl.ds(pl.multiple_of(at * wide, 128), wide)

    def piece(i, shard, quarter):
        return pairs[i][1].at[pl.ds(pl.multiple_of(shard * rows + quarter * part, 16), part)]

    def w_copy(i, stage, k, src, dst, device):
        return remote(src, dst, w_send.at[stage, i, k], w_recv.at[stage, i, k], device)

    def own_row(j):
        return ((a + line - j) % line) * 2 + b

    def other_row(j):
        return ((a + line - j) % line) * 2 + 1 - b

    def h_copy(sems, j, src, dst, device):
        return remote(src, dst, sems[0].at[j], sems[1].at[j], device)

    zs, ys, xs, gs = (z_send, z_recv), (y_send, y_recv), (x_send, x_recv), (g_send, g_recv)

    def core(kind, j, src, dst):
        return remote(src, dst, c_send.at[kind, j], c_recv.at[kind, j], to_c)

    def z_first(j, carry):
        target = ((a + j) % line) * 2 + b
        h_copy(zs, j, n_ref, hid_ref.at[0, f], {"fsdp": target}).start()
        return carry

    h_copy(ys, 0, n_ref, hid_ref.at[0, f], to_y).start()
    h_copy(xs, 0, n_ref, hid_ref.at[2, f], to_x).start()
    core(0, 0, n_ref, hid_ref.at[1, f]).start()
    lax.fori_loop(1, line, z_first, 0)

    def w_first(k, carry):
        target = (f + k) % count
        for i in range(2):
            src = pairs[i][0].at[pl.ds(pl.multiple_of(mine * part, 16), part), columns(i, target)]
            w_copy(i, 0, k, src, piece(i, f, mine), {"fsdp": target}).start()
        return carry

    lax.fori_loop(1, count, w_first, 0)
    locals_ = [pltpu.make_async_copy(n_ref, hid_ref.at[0, f], own_sem.at[0])]
    for i in range(2):
        dst = pairs[i][1].at[pl.ds(pl.multiple_of(f * rows, 16), rows)]
        locals_.append(pltpu.make_async_copy(pairs[i][0].at[:, columns(i, f)], dst, own_sem.at[1 + i]))
    for copy in locals_:
        copy.start()

    def z_next(j, carry):
        at = hid_ref.at[0, own_row(j)]
        h_copy(zs, j, at, at, to_y).wait_recv()
        h_copy(ys, j, at, at, to_y).start()
        h_copy(xs, j, at, hid_ref.at[2, own_row(j)], to_x).start()
        core(0, j, at, hid_ref.at[1, own_row(j)]).start()
        return carry

    lax.fori_loop(1, line, z_next, 0)

    def w_next(k, carry):
        for i in range(2):
            at = piece(i, (f + count - k) % count, mine)
            w_copy(i, 0, k, at, at, to_x).wait_recv()
            w_copy(i, 1, k, at, at, to_x).start()
            w_copy(i, 2, k, at, at, to_c).start()
        return carry

    def y_next(j, via):
        at = hid_ref.at[0, other_row(j)]
        h_copy(ys, j, at, at, to_y).wait_recv()
        core(1, j, at, hid_ref.at[1, other_row(j)]).start()
        if via:
            h_copy(gs, j, at, hid_ref.at[2, other_row(j)], to_x).start()

    def x_next(j, via):
        at = hid_ref.at[2, own_row(j)]
        h_copy(xs, j, at, at, to_x).wait_recv()
        core(2, j, at, hid_ref.at[3, own_row(j)]).start()
        if not via:
            h_copy(gs, j, at, at, to_y).start()

    def both(via, j, carry):
        y_next(j, via)
        x_next(j, via)
        return carry

    half = (count + 1) // 2
    lax.fori_loop(1, half, w_next, 0)
    lax.fori_loop(0, via_x, functools.partial(both, True), 0)
    lax.fori_loop(via_x, line, functools.partial(both, False), 0)
    lax.fori_loop(half, count, w_next, 0)

    def w_last(k, carry):
        for i in range(2):
            at = piece(i, (f + count - k) % count, across)
            w_copy(i, 1, k, at, at, to_x).wait_recv()
            w_copy(i, 3, k, at, at, to_c).start()
        return carry

    lax.fori_loop(1, count, w_last, 0)

    def g_last(j, carry):
        at = hid_ref.at[2, other_row(j)]
        h_copy(gs, j, at, at, to_x).wait_recv()
        core(3, j, at, hid_ref.at[3, other_row(j)]).start()
        return carry

    lax.fori_loop(0, line, g_last, 0)

    def w_end(k, carry):
        shard = (f + count - k) % count
        for i in range(2):
            near, far = piece(i, shard, s * 2 + 1 - d), piece(i, shard, (1 - s) * 2 + 1 - d)
            w_copy(i, 2, k, near, near, to_c).wait_recv()
            w_copy(i, 3, k, far, far, to_c).wait_recv()
            for stage in range(4):
                w_copy(i, stage, k, near, near, to_c).wait_send()
        return carry

    lax.fori_loop(1, count, w_end, 0)

    def h_end(j, carry):
        for kind, block, place in ((0, 1, own_row(j)), (1, 1, other_row(j)), (2, 3, own_row(j)), (3, 3, other_row(j))):
            at = hid_ref.at[block, place]
            core(kind, j, at, at).wait_recv()
            core(kind, j, at, at).wait_send()
        for sems in (ys, xs, gs):
            h_copy(sems, j, n_ref, n_ref, to_y).wait_send()
        return carry

    lax.fori_loop(0, line, h_end, 0)

    def z_end(j, carry):
        h_copy(zs, j, n_ref, n_ref, to_y).wait_send()
        return carry

    lax.fori_loop(1, line, z_end, 0)
    for copy in locals_:
        copy.wait()


def gather_all(count, share, normed, w_query, wkv):
    line = count // 2
    rows, width = normed.shape
    dma = pltpu.SemaphoreType.DMA
    pair = lambda *shape: [dma(shape), dma(shape)]
    out = lambda *shape: jax.ShapeDtypeStruct(shape, jnp.bfloat16)
    kv_wide = wkv.shape[1] // min(count, KVH)
    return pl.pallas_call(
        functools.partial(gather_kernel, count, share),
        out_shape=(
            out(4, count, rows, width),
            out(count * w_query.shape[0], w_query.shape[1] // count),
            out(count * wkv.shape[0], kv_wide),
        ),
        in_specs=[pl.BlockSpec(memory_space=pl.ANY)] * 3,
        out_specs=[pl.BlockSpec(memory_space=pl.ANY)] * 3,
        scratch_shapes=pair(4, 2, count) + pair(line) * 4 + pair(4, line) + [dma((3,))],
        compiler_params=pltpu.CompilerParams(collective_id=0, has_side_effects=True),
        name="gather_all",
    )(normed, w_query, wkv)


def exchange_kernel(q_ref, kv_ref, q_all, kv_all, send, recv, own_sem):
    s, d = lax.axis_index("section"), lax.axis_index("dp")
    to_x, to_c = {"section": 1 - s}, {"dp": 1 - d}
    barrier = pltpu.get_barrier_semaphore()
    pl.semaphore_signal(barrier, inc=1, device_id=to_x, device_id_type=MESH)
    pl.semaphore_signal(barrier, inc=1, device_id=to_c, device_id_type=MESH)
    pl.semaphore_wait(barrier, 2)
    pairs = ((q_ref, q_all), (kv_ref, kv_all))
    waits = []
    for i, (src, dst) in enumerate(pairs):
        over = remote(src, dst.at[2], send.at[i, 0], recv.at[i, 0], to_x)
        near = remote(src, dst.at[1], send.at[i, 1], recv.at[i, 1], to_c)
        own = pltpu.make_async_copy(src, dst.at[0], own_sem.at[i])
        for copy in (over, near, own):
            copy.start()
        waits.append((over, near, own))
    lasts = []
    for i, (src, dst) in enumerate(pairs):
        waits[i][0].wait_recv()
        last = remote(dst.at[2], dst.at[3], send.at[i, 2], recv.at[i, 2], to_c)
        last.start()
        lasts.append(last)
    for i in range(2):
        waits[i][0].wait_send()
        waits[i][1].wait()
        waits[i][2].wait()
        lasts[i].wait()


def exchange(scaled_q, scaled_kv):
    dma = pltpu.SemaphoreType.DMA
    out = lambda x: jax.ShapeDtypeStruct((4,) + x.shape, jnp.bfloat16)
    return pl.pallas_call(
        exchange_kernel,
        out_shape=(out(scaled_q), out(scaled_kv)),
        in_specs=[pl.BlockSpec(memory_space=pl.ANY)] * 2,
        out_specs=[pl.BlockSpec(memory_space=pl.ANY)] * 2,
        scratch_shapes=[dma((2, 3)), dma((2, 3)), dma((2,))],
        compiler_params=pltpu.CompilerParams(collective_id=1, has_side_effects=True),
        name="exchange",
    )(scaled_q, scaled_kv)


def local(hidden, cotangent, seg_ids, advantage, w_query, w_key, w_value):
    fsdp_size = lax.axis_size("fsdp")
    share_count = max(1, fsdp_size // KVH)
    kv_local = max(1, KVH // fsdp_size)
    heads_local = H // fsdp_size
    per_copy = heads_local // kv_local
    inv_width = D ** (-0.5)

    rows = hidden[0].astype(jnp.float32)
    own_normed = (
        rows * lax.rsqrt(jnp.mean(rows * rows, axis=-1, keepdims=True) + norm_eps)
    ).astype(jnp.bfloat16)
    width_rows = w_key.shape[0]
    groups = KVH // kv_local
    wkv = jnp.concatenate(
        [
            w_key.reshape(width_rows, groups, kv_local * HD),
            w_value.reshape(width_rows, groups, kv_local * HD),
        ],
        axis=2,
    ).reshape(width_rows, 2 * KVH * HD)
    normed_all, q_cols, kv_cols = gather_all(fsdp_size, share_count, own_normed, w_query, wkv)
    normed_all = normed_all.reshape(4, -1, D)
    normed = normed_all[0]
    block_len = normed.shape[0]
    queries = jnp.dot(normed, q_cols, preferred_element_type=jnp.float32) * inv_width
    kv_proj = jnp.dot(normed, kv_cols, preferred_element_type=jnp.float32) * inv_width
    key_proj, value_proj = kv_proj[:, : kv_local * HD], kv_proj[:, kv_local * HD :]
    seg_row = seg_ids[0]
    cosine_table, sine_table = angles(seg_row)
    q_rot = rotate(queries.reshape(block_len, heads_local, HD), cosine_table, sine_table).astype(
        jnp.bfloat16
    )
    k_rot = rotate(key_proj.reshape(block_len, kv_local, HD), cosine_table, sine_table).astype(
        jnp.bfloat16
    )
    v_bf = value_proj.astype(jnp.bfloat16).reshape(block_len, kv_local, HD)
    weight_row = token_weights(seg_row, advantage[0])
    grad_context = (cotangent[0].astype(jnp.float32) * weight_row[:, None]).astype(jnp.bfloat16)
    place = jnp.arange(block_len, dtype=jnp.int32)
    allowed = (seg_row[:, None] == seg_row[None, :]) & (place[None, :] <= place[:, None])
    grad_query, grad_key, grad_value = attend_back(
        q_rot.reshape(block_len, kv_local, 1, per_copy, HD),
        k_rot,
        v_bf,
        grad_context.reshape(block_len, kv_local, 1, per_copy, HD),
        allowed,
    )
    grad_query = unrotate(grad_query.reshape(block_len, heads_local, HD), cosine_table, sine_table)
    grad_key = unrotate(grad_key.reshape(block_len, kv_local, HD), cosine_table, sine_table)
    scaled_q = (grad_query.reshape(block_len, heads_local * HD) * inv_width).astype(jnp.bfloat16)
    scaled_k = (grad_key.reshape(block_len, kv_local * HD) * inv_width).astype(jnp.bfloat16)
    scaled_v = (grad_value.reshape(block_len, kv_local * HD) * inv_width).astype(jnp.bfloat16)
    all_q, all_kv = exchange(scaled_q, jnp.concatenate([scaled_k, scaled_v], axis=1))
    contract = (((0, 1), (0, 1)), ((), ()))
    total_q = lax.dot_general(normed_all, all_q, contract, preferred_element_type=jnp.float32)
    total_kv = lax.dot_general(normed_all, all_kv, contract, preferred_element_type=jnp.float32)
    new_q = (q_cols.astype(jnp.float32) - step_rate * total_q).astype(jnp.bfloat16)
    new_kv = (kv_cols.astype(jnp.float32) - step_rate * total_kv).astype(jnp.bfloat16)
    return (new_q, new_kv[:, : kv_local * HD], new_kv[:, kv_local * HD :])


def solution(mesh):
    in_specs = (
        P(("section", "dp"), "fsdp", None),
        P(("section", "dp"), None, "fsdp"),
        P(("section", "dp"), None),
        P(("section", "dp"), None),
        P("fsdp", None),
        P("fsdp", None),
        P("fsdp", None),
    )
    out_specs = (P(None, "fsdp"), P(None, "fsdp"), P(None, "fsdp"))
    return jax.shard_map(local, mesh=mesh, in_specs=in_specs, out_specs=out_specs, check_vma=False)
```

```python
import functools

import jax
import jax.numpy as jnp
from jax import lax
from jax.experimental import pallas as pl
from jax.experimental.pallas import tpu as pltpu
from jax.sharding import PartitionSpec as P

D = 8192
H = 64
KVH = 8
HD = 128
RESP = 8


step_rate = 200.0
rope_base = 1000000.0
norm_eps = 1e-06
masked_score = -1e30


def rotate(field, cosine_table, sine_table):
    half_width = field.shape[-1] // 2
    lead_half = field[..., :half_width]
    tail_half = field[..., half_width:]
    return jnp.concatenate(
        [
            lead_half * cosine_table - tail_half * sine_table,
            tail_half * cosine_table + lead_half * sine_table,
        ],
        -1,
    )


def unrotate(field, cosine_table, sine_table):
    half_width = field.shape[-1] // 2
    lead_half = field[..., :half_width]
    tail_half = field[..., half_width:]
    return jnp.concatenate(
        [
            lead_half * cosine_table + tail_half * sine_table,
            tail_half * cosine_table - lead_half * sine_table,
        ],
        -1,
    )


def angles(seg_row):
    span_count = seg_row.shape[0]
    earlier = jnp.sum((seg_row[None, :] < seg_row[:, None]).astype(jnp.int32), axis=1)
    positions = jnp.arange(span_count, dtype=jnp.int32) - earlier
    frequency = rope_base ** (-jnp.arange(HD // 2, dtype=jnp.float32) * 2.0 / HD)
    phase_grid = positions.astype(jnp.float32)[:, None] * frequency[None, :]
    return (jnp.cos(phase_grid)[:, None, :], jnp.sin(phase_grid)[:, None, :])


def token_weights(seg_row, advantage_row):
    id_range = jnp.arange(RESP + 1, dtype=jnp.int32)
    onehot = (seg_row[:, None] == id_range[None, :]).astype(jnp.float32)
    counts = jnp.sum(onehot, axis=0)[:RESP]
    per_token = -advantage_row / counts
    return jnp.sum(onehot[:, :RESP] * per_token[None, :], axis=1)


def attend_back(q_rot, k_rot, v_bf, grad_context, allowed):
    score_scale = HD ** (-0.5)
    scores = (
        jnp.einsum("tkjqd,ukd->kjqtu", q_rot, k_rot, preferred_element_type=jnp.float32)
        * score_scale
    )
    scores = jnp.where(allowed, scores, masked_score)
    row_top = jnp.max(scores, axis=-1, keepdims=True)
    exponent = jnp.exp(scores - row_top)
    attention = exponent / jnp.sum(exponent, axis=-1, keepdims=True)
    attention_bf = attention.astype(jnp.bfloat16)
    grad_prob = jnp.einsum(
        "tkjqd,ukd->kjqtu", grad_context, v_bf, preferred_element_type=jnp.float32
    )
    inner_sum = jnp.sum(attention * grad_prob, axis=-1, keepdims=True)
    dscore = (attention * (grad_prob - inner_sum)).astype(jnp.bfloat16)
    grad_query = (
        jnp.einsum("kjqtu,ukd->tkjqd", dscore, k_rot, preferred_element_type=jnp.float32)
        * score_scale
    )
    grad_key = (
        jnp.einsum("kjqtu,tkjqd->ukjd", dscore, q_rot, preferred_element_type=jnp.float32)
        * score_scale
    )
    grad_value = jnp.einsum(
        "kjqtu,tkjqd->ukjd", attention_bf, grad_context, preferred_element_type=jnp.float32
    )
    return (grad_query, grad_key, grad_value)

MESH = pl.DeviceIdType.MESH


def remote(src, dst, send, recv, device):
    return pltpu.make_async_remote_copy(
        src_ref=src, dst_ref=dst, send_sem=send, recv_sem=recv, device_id=device, device_id_type=MESH
    )


def gather_kernel(
    count, share, n_ref, wq_ref, wkv_ref, hid_ref, qc_ref, kv_ref,
    w_send, w_recv, z_send, z_recv, y_send, y_recv, x_send, x_recv, g_send, g_recv, c_send, c_recv,
    own_sem,
):
    s, f, d = lax.axis_index("section"), lax.axis_index("fsdp"), lax.axis_index("dp")
    line = count // 2
    a, b = f // 2, f % 2
    to_y, to_x, to_c = {"fsdp": a * 2 + 1 - b}, {"section": 1 - s}, {"dp": 1 - d}
    rows = wq_ref.shape[0]
    part = rows // 4
    mine, across = s * 2 + d, (1 - s) * 2 + d
    pairs = ((wq_ref, qc_ref), (wkv_ref, kv_ref))
    via_x = line // 4

    barrier = pltpu.get_barrier_semaphore()

    def greet(k, carry):
        pl.semaphore_signal(barrier, inc=1, device_id={"fsdp": (f + k) % count}, device_id_type=MESH)
        return carry

    lax.fori_loop(1, count, greet, 0)
    pl.semaphore_signal(barrier, inc=1, device_id=to_x, device_id_type=MESH)
    pl.semaphore_signal(barrier, inc=1, device_id=to_c, device_id_type=MESH)
    pl.semaphore_wait(barrier, count + 1)

    def columns(i, target):
        wide = pairs[i][1].shape[1]
        at = target if i == 0 else target // share
        return pl.ds(pl.multiple_of(at * wide, 128), wide)

    def piece(i, shard, quarter):
        return pairs[i][1].at[pl.ds(pl.multiple_of(shard * rows + quarter * part, 16), part)]

    def w_copy(i, stage, k, src, dst, device):
        return remote(src, dst, w_send.at[stage, i, k], w_recv.at[stage, i, k], device)

    def own_row(j):
        return ((a + line - j) % line) * 2 + b

    def other_row(j):
        return ((a + line - j) % line) * 2 + 1 - b

    def h_copy(sems, j, src, dst, device):
        return remote(src, dst, sems[0].at[j], sems[1].at[j], device)

    zs, ys, xs, gs = (z_send, z_recv), (y_send, y_recv), (x_send, x_recv), (g_send, g_recv)

    def core(kind, j, src, dst):
        return remote(src, dst, c_send.at[kind, j], c_recv.at[kind, j], to_c)

    def z_first(j, carry):
        target = ((a + j) % line) * 2 + b
        h_copy(zs, j, n_ref, hid_ref.at[0, f], {"fsdp": target}).start()
        return carry

    h_copy(ys, 0, n_ref, hid_ref.at[0, f], to_y).start()
    h_copy(xs, 0, n_ref, hid_ref.at[2, f], to_x).start()
    core(0, 0, n_ref, hid_ref.at[1, f]).start()
    lax.fori_loop(1, line, z_first, 0)

    def w_first(k, carry):
        target = (f + k) % count
        for i in range(2):
            src = pairs[i][0].at[pl.ds(pl.multiple_of(mine * part, 16), part), columns(i, target)]
            w_copy(i, 0, k, src, piece(i, f, mine), {"fsdp": target}).start()
        return carry

    lax.fori_loop(1, count, w_first, 0)
    locals_ = [pltpu.make_async_copy(n_ref, hid_ref.at[0, f], own_sem.at[0])]
    for i in range(2):
        dst = pairs[i][1].at[pl.ds(pl.multiple_of(f * rows, 16), rows)]
        locals_.append(pltpu.make_async_copy(pairs[i][0].at[:, columns(i, f)], dst, own_sem.at[1 + i]))
    for copy in locals_:
        copy.start()

    def z_next(j, carry):
        at = hid_ref.at[0, own_row(j)]
        h_copy(zs, j, at, at, to_y).wait_recv()
        h_copy(ys, j, at, at, to_y).start()
        h_copy(xs, j, at, hid_ref.at[2, own_row(j)], to_x).start()
        core(0, j, at, hid_ref.at[1, own_row(j)]).start()
        return carry

    lax.fori_loop(1, line, z_next, 0)

    def w_next(k, carry):
        for i in range(2):
            at = piece(i, (f + count - k) % count, mine)
            w_copy(i, 0, k, at, at, to_x).wait_recv()
            w_copy(i, 1, k, at, at, to_x).start()
            w_copy(i, 2, k, at, at, to_c).start()
        return carry

    def y_next(j, via):
        at = hid_ref.at[0, other_row(j)]
        h_copy(ys, j, at, at, to_y).wait_recv()
        core(1, j, at, hid_ref.at[1, other_row(j)]).start()
        if via:
            h_copy(gs, j, at, hid_ref.at[2, other_row(j)], to_x).start()

    def x_next(j, via):
        at = hid_ref.at[2, own_row(j)]
        h_copy(xs, j, at, at, to_x).wait_recv()
        core(2, j, at, hid_ref.at[3, own_row(j)]).start()
        if not via:
            h_copy(gs, j, at, at, to_y).start()

    def both(via, j, carry):
        y_next(j, via)
        x_next(j, via)
        w_next(2 * j + 1, 0)

        @pl.when(2 * j + 2 < count)
        def _():
            w_next(2 * j + 2, 0)

        return carry

    lax.fori_loop(0, via_x, functools.partial(both, True), 0)
    lax.fori_loop(via_x, line, functools.partial(both, False), 0)

    def w_last(k, carry):
        for i in range(2):
            at = piece(i, (f + count - k) % count, across)
            w_copy(i, 1, k, at, at, to_x).wait_recv()
            w_copy(i, 3, k, at, at, to_c).start()
        return carry

    lax.fori_loop(1, count, w_last, 0)

    def g_last(j, carry):
        at = hid_ref.at[2, other_row(j)]
        h_copy(gs, j, at, at, to_x).wait_recv()
        core(3, j, at, hid_ref.at[3, other_row(j)]).start()
        return carry

    lax.fori_loop(0, line, g_last, 0)

    def w_end(k, carry):
        shard = (f + count - k) % count
        for i in range(2):
            near, far = piece(i, shard, s * 2 + 1 - d), piece(i, shard, (1 - s) * 2 + 1 - d)
            w_copy(i, 2, k, near, near, to_c).wait_recv()
            w_copy(i, 3, k, far, far, to_c).wait_recv()
            for stage in range(4):
                w_copy(i, stage, k, near, near, to_c).wait_send()
        return carry

    lax.fori_loop(1, count, w_end, 0)

    def h_end(j, carry):
        for kind, block, place in ((0, 1, own_row(j)), (1, 1, other_row(j)), (2, 3, own_row(j)), (3, 3, other_row(j))):
            at = hid_ref.at[block, place]
            core(kind, j, at, at).wait_recv()
            core(kind, j, at, at).wait_send()
        for sems in (ys, xs, gs):
            h_copy(sems, j, n_ref, n_ref, to_y).wait_send()
        return carry

    lax.fori_loop(0, line, h_end, 0)

    def z_end(j, carry):
        h_copy(zs, j, n_ref, n_ref, to_y).wait_send()
        return carry

    lax.fori_loop(1, line, z_end, 0)
    for copy in locals_:
        copy.wait()


def gather_all(count, share, normed, w_query, wkv):
    line = count // 2
    rows, width = normed.shape
    dma = pltpu.SemaphoreType.DMA
    pair = lambda *shape: [dma(shape), dma(shape)]
    out = lambda *shape: jax.ShapeDtypeStruct(shape, jnp.bfloat16)
    kv_wide = wkv.shape[1] // min(count, KVH)
    return pl.pallas_call(
        functools.partial(gather_kernel, count, share),
        out_shape=(
            out(4, count, rows, width),
            out(count * w_query.shape[0], w_query.shape[1] // count),
            out(count * wkv.shape[0], kv_wide),
        ),
        in_specs=[pl.BlockSpec(memory_space=pl.ANY)] * 3,
        out_specs=[pl.BlockSpec(memory_space=pl.ANY)] * 3,
        scratch_shapes=pair(4, 2, count) + pair(line) * 4 + pair(4, line) + [dma((3,))],
        compiler_params=pltpu.CompilerParams(collective_id=0, has_side_effects=True),
        name="gather_all",
    )(normed, w_query, wkv)


def project_kernel(n_ref, wq_ref, wkv_ref, q_ref, kv_ref):
    @pl.when(pl.program_id(0) == 0)
    def _():
        q_ref[...] = jnp.zeros_like(q_ref)
        kv_ref[...] = jnp.zeros_like(kv_ref)

    normed = n_ref[0]
    q_ref[...] += jnp.dot(normed, wq_ref[...], preferred_element_type=jnp.float32)
    kv_ref[...] += jnp.dot(normed, wkv_ref[...], preferred_element_type=jnp.float32)


def project(normed_all, q_cols, kv_cols):
    _, block_len, width = normed_all.shape
    step = min(1024, width)
    q_wide, kv_wide = q_cols.shape[1], kv_cols.shape[1]
    return pl.pallas_call(
        project_kernel,
        grid=(width // step,),
        in_specs=[
            pl.BlockSpec((1, block_len, step), lambda k: (0, 0, k)),
            pl.BlockSpec((step, q_wide), lambda k: (k, 0)),
            pl.BlockSpec((step, kv_wide), lambda k: (k, 0)),
        ],
        out_specs=[
            pl.BlockSpec((block_len, q_wide), lambda k: (0, 0)),
            pl.BlockSpec((block_len, kv_wide), lambda k: (0, 0)),
        ],
        out_shape=[
            jax.ShapeDtypeStruct((block_len, q_wide), jnp.float32),
            jax.ShapeDtypeStruct((block_len, kv_wide), jnp.float32),
        ],
        compiler_params=pltpu.CompilerParams(vmem_limit_bytes=32 * 1024 * 1024),
        name="project",
    )(normed_all, q_cols, kv_cols)


def exchange_kernel(q_ref, kv_ref, q_all, kv_all, send, recv, own_sem):
    s, d = lax.axis_index("section"), lax.axis_index("dp")
    to_x, to_c = {"section": 1 - s}, {"dp": 1 - d}
    barrier = pltpu.get_barrier_semaphore()
    pl.semaphore_signal(barrier, inc=1, device_id=to_x, device_id_type=MESH)
    pl.semaphore_signal(barrier, inc=1, device_id=to_c, device_id_type=MESH)
    pl.semaphore_wait(barrier, 2)
    pairs = ((q_ref, q_all), (kv_ref, kv_all))
    waits = []
    for i, (src, dst) in enumerate(pairs):
        over = remote(src, dst.at[2], send.at[i, 0], recv.at[i, 0], to_x)
        near = remote(src, dst.at[1], send.at[i, 1], recv.at[i, 1], to_c)
        own = pltpu.make_async_copy(src, dst.at[0], own_sem.at[i])
        for copy in (over, near, own):
            copy.start()
        waits.append((over, near, own))
    lasts = []
    for i, (src, dst) in enumerate(pairs):
        waits[i][0].wait_recv()
        last = remote(dst.at[2], dst.at[3], send.at[i, 2], recv.at[i, 2], to_c)
        last.start()
        lasts.append(last)
    for i in range(2):
        waits[i][0].wait_send()
        waits[i][1].wait()
        waits[i][2].wait()
        lasts[i].wait()


def exchange(scaled_q, scaled_kv):
    dma = pltpu.SemaphoreType.DMA
    out = lambda x: jax.ShapeDtypeStruct((4,) + x.shape, jnp.bfloat16)
    return pl.pallas_call(
        exchange_kernel,
        out_shape=(out(scaled_q), out(scaled_kv)),
        in_specs=[pl.BlockSpec(memory_space=pl.ANY)] * 2,
        out_specs=[pl.BlockSpec(memory_space=pl.ANY)] * 2,
        scratch_shapes=[dma((2, 3)), dma((2, 3)), dma((2,))],
        compiler_params=pltpu.CompilerParams(collective_id=1, has_side_effects=True),
        name="exchange",
    )(scaled_q, scaled_kv)


def local(hidden, cotangent, seg_ids, advantage, w_query, w_key, w_value):
    fsdp_size = lax.axis_size("fsdp")
    share_count = max(1, fsdp_size // KVH)
    kv_local = max(1, KVH // fsdp_size)
    heads_local = H // fsdp_size
    per_copy = heads_local // kv_local
    inv_width = D ** (-0.5)

    rows = hidden[0].astype(jnp.float32)
    own_normed = (
        rows * lax.rsqrt(jnp.mean(rows * rows, axis=-1, keepdims=True) + norm_eps)
    ).astype(jnp.bfloat16)
    width_rows = w_key.shape[0]
    groups = KVH // kv_local
    wkv = jnp.concatenate(
        [
            w_key.reshape(width_rows, groups, kv_local * HD),
            w_value.reshape(width_rows, groups, kv_local * HD),
        ],
        axis=2,
    ).reshape(width_rows, 2 * KVH * HD)
    normed_all, q_cols, kv_cols = gather_all(fsdp_size, share_count, own_normed, w_query, wkv)
    normed_all = normed_all.reshape(4, -1, D)
    block_len = normed_all.shape[1]
    queries, kv_proj = (out * inv_width for out in project(normed_all, q_cols, kv_cols))
    key_proj, value_proj = kv_proj[:, : kv_local * HD], kv_proj[:, kv_local * HD :]
    seg_row = seg_ids[0]
    cosine_table, sine_table = angles(seg_row)
    q_rot = rotate(queries.reshape(block_len, heads_local, HD), cosine_table, sine_table).astype(
        jnp.bfloat16
    )
    k_rot = rotate(key_proj.reshape(block_len, kv_local, HD), cosine_table, sine_table).astype(
        jnp.bfloat16
    )
    v_bf = value_proj.astype(jnp.bfloat16).reshape(block_len, kv_local, HD)
    weight_row = token_weights(seg_row, advantage[0])
    grad_context = (cotangent[0].astype(jnp.float32) * weight_row[:, None]).astype(jnp.bfloat16)
    place = jnp.arange(block_len, dtype=jnp.int32)
    allowed = (seg_row[:, None] == seg_row[None, :]) & (place[None, :] <= place[:, None])
    grad_query, grad_key, grad_value = attend_back(
        q_rot.reshape(block_len, kv_local, 1, per_copy, HD),
        k_rot,
        v_bf,
        grad_context.reshape(block_len, kv_local, 1, per_copy, HD),
        allowed,
    )
    grad_query = unrotate(grad_query.reshape(block_len, heads_local, HD), cosine_table, sine_table)
    grad_key = unrotate(grad_key.reshape(block_len, kv_local, HD), cosine_table, sine_table)
    scaled_q = (grad_query.reshape(block_len, heads_local * HD) * inv_width).astype(jnp.bfloat16)
    scaled_k = (grad_key.reshape(block_len, kv_local * HD) * inv_width).astype(jnp.bfloat16)
    scaled_v = (grad_value.reshape(block_len, kv_local * HD) * inv_width).astype(jnp.bfloat16)
    all_q, all_kv = exchange(scaled_q, jnp.concatenate([scaled_k, scaled_v], axis=1))
    contract = (((0, 1), (0, 1)), ((), ()))
    total_q = lax.dot_general(normed_all, all_q, contract, preferred_element_type=jnp.float32)
    total_kv = lax.dot_general(normed_all, all_kv, contract, preferred_element_type=jnp.float32)
    new_q = (q_cols.astype(jnp.float32) - step_rate * total_q).astype(jnp.bfloat16)
    new_kv = (kv_cols.astype(jnp.float32) - step_rate * total_kv).astype(jnp.bfloat16)
    return (new_q, new_kv[:, : kv_local * HD], new_kv[:, kv_local * HD :])


def solution(mesh):
    in_specs = (
        P(("section", "dp"), "fsdp", None),
        P(("section", "dp"), None, "fsdp"),
        P(("section", "dp"), None),
        P(("section", "dp"), None),
        P("fsdp", None),
        P("fsdp", None),
        P("fsdp", None),
    )
    out_specs = (P(None, "fsdp"), P(None, "fsdp"), P(None, "fsdp"))
    return jax.shard_map(local, mesh=mesh, in_specs=in_specs, out_specs=out_specs, check_vma=False)
```
